32 devices in a mesh: groups: 2 (over y), tensor: 4 (over z), adapter: 2 (over x), dp: 2 (over core).
Axes of the slice: x: 2, y: 2, z: 4, core: 2. Of those that a mesh axis runs over, the one named last changes fastest.
Arguments:
- tokens: bfloat16 [1024, 8192], P(('groups', 'adapter', 'dp'), 'tensor'), parts along dimension 0, may hold values from -6 to 6
- base_projection_weight: bfloat16 [8192, 2048], P(None, 'tensor'), may hold values from -0.0625 to 0.0625
- adapter_down_weight: bfloat16 [4, 8192, 64], P('adapter', 'tensor'), may hold values from -0.0625 to 0.0625
- adapter_up_weight: bfloat16 [4, 64, 2048], P('adapter', None, 'tensor'), may hold values from -0.75 to 0.75
- token_row_adapter: int32 [1024, 1], P(('groups', 'adapter', 'dp')), parts along dimension 0, may hold values from 0 to 3; in each aligned block of 128 rows (0 to 127, 128 to 255, ...) at most 128 rows name the same one
- adapter_slot_table: int32 [4], replicated, may hold values from 0 to 3, each once
Outputs:
- key_value: bfloat16 [1024, 2048], P(('groups', 'adapter', 'dp'), 'tensor'), parts along dimension 0
The draws below stay inside these ranges and needn't reach their ends.
There are 2 independent parts, one for each index of `groups`. The reference program is written for one: setup_inputs(seed, part) draws one part's arguments, and reference() takes and returns one part's arrays. A program takes and returns all parts, laid end to end along the dimension named above; an argument that names none is the same for every part. Nothing has to cross between parts.
Inputs may be any that keep to these rules, and one draw needn't show every extreme that they name: `token_row_adapter`: among the 128 rows of one index of adapter+dp, no adapter id is named by more than 128 rows; in some of these blocks one is named by exactly 128; every id is named somewhere. `adapter_slot_table`: each slot once; slot s is stored on index s // 2 of adapter.
All inputs are finite; a program needn't handle non-finite values.
Results may differ from the reference program's by a relative error of at most 0.0035.
Values may be sent and summed in bfloat16 or wider, within the bound.
A program may use at most 64 MiB of HBM per device.

```python
import math
import jax
import jax.numpy as jnp
import numpy as np
from jax import lax

MODEL_WIDTH = 8192
KEY_VALUE_WIDTH = 1024
ADAPTER_RANK = 64
CAP = 128
ROWS_COL = 128
ADAPTER_TOTAL = 4
TOKENS = 512


def shard_levels(rng, extent, cuts, low, top_value):
    level, own = 1.0, jax.random.fold_in(rng, 6)
    for dim, shards_of in cuts:
        heights = jnp.exp(jax.random.uniform(jax.random.fold_in(own, dim), (shards_of,), jnp.float32, low / len(cuts), top_value / len(cuts)))
        level = level * jnp.repeat(heights, extent[dim] // shards_of).reshape([-1 if axis == dim else 1 for axis in range(len(extent))])
    return level


def shared_out(stream_key, own, number, rows, number_of, top, limit, slope):
    sequence = jax.random.permutation(stream_key, number_of)
    heavy_load, common = portions_of(number_of, rows * top, limit, slope, True), portions_of(number_of, rows * top, limit, slope, False)
    places = jnp.arange(number_of)

    def named(sizes, turn):
        used = int((sizes > 0).sum())
        fixed = max(1, used // 4)
        moved = fixed + (places - fixed + turn * (used - fixed)) % max(1, number_of - fixed)
        return jnp.zeros((number_of,), jnp.int32).at[sequence[jnp.where(places < fixed, places, moved)]].set(jnp.asarray(sizes, jnp.int32))

    sizes = jnp.where(number % 4 == 0, named(heavy_load, number // 4), named(common, number - number // 4 - 1))
    mixed = jax.random.permutation(jax.random.fold_in(own, 3), number_of)
    source_of, sink = mixed[0:number_of // 2 * 2:2], mixed[1:number_of // 2 * 2:2]
    slack = jnp.minimum(sizes[source_of] - 1, limit - sizes[sink]) // 2
    slack = jnp.where((source_of == sequence[0]) | (sink == sequence[0]) | (sizes[sink] == 0), 0, jnp.maximum(slack, 0))
    moved = jax.random.randint(jax.random.fold_in(own, 4), (number_of // 2,), 0, 1 << 20) % (slack + 1)
    sizes = sizes.at[source_of].add(-moved).at[sink].add(moved)
    labels = jnp.searchsorted(jnp.cumsum(sizes), jnp.arange(rows * top), side="right").astype(jnp.int32)
    grid = labels.reshape(top, rows).T
    grid = grid[jax.random.permutation(jax.random.fold_in(own, 1), rows)]
    turn = jax.random.randint(jax.random.fold_in(own, 2), (rows, 1), 0, top)
    return jnp.take_along_axis(grid, (jnp.arange(top)[None, :] + turn) % top, axis=1)


def portions_of(count, total, most, slope, full):
    portions = [(1 << 20) // math.isqrt(standing ** slope) + 1 for standing in range(1, count + 1)]
    largest = most if full else min(most, max(-(-total // count), total * portions[0] // sum(portions)))
    least = 1 if total - largest >= count - 1 else 0
    counts, spare = [largest] + [least] * (count - 1), total - largest - least * (count - 1)
    while spare > 0:
        movable = [i for i in range(1, count) if counts[i] < largest] or [i for i in range(1, count) if counts[i] < most]
        mass, remaining = sum([portions[i] for i in movable]), spare
        for i in movable:
            extra = min(most - counts[i], max(1, remaining * portions[i] // mass), spare)
            counts[i] = counts[i] + extra
            spare = spare - extra
    return np.array(counts)


def bell_draw(rng, dims, deviation, reach, split=(), kind=jnp.bfloat16):
    loudness = shard_levels(rng, dims, split, -0.22, 0.18) if split else 1.0
    result = jax.random.normal(rng, dims, jnp.float32) * deviation * loudness
    return jnp.minimum(jnp.maximum(result, -reach), reach).astype(kind)


def setup_inputs(seed: int = 0, part: int = 0) -> dict:
    arg_keys = jax.random.split(jax.random.key(seed), 7)
    own_keys = jax.random.split(jax.random.fold_in(arg_keys[6], part), 7)
    tokens = bell_draw(own_keys[0], (TOKENS, MODEL_WIDTH), 1.0, 6.0, ((0, 4), (1, 4)))
    base_projection_weight = bell_draw(arg_keys[1], (MODEL_WIDTH, 2 * KEY_VALUE_WIDTH), MODEL_WIDTH ** -0.5, 0.0625, ((1, 4),))
    adapter_down_weight = bell_draw(arg_keys[2], (ADAPTER_TOTAL, MODEL_WIDTH, ADAPTER_RANK), MODEL_WIDTH ** -0.5, 0.0625, ((0, 2), (1, 4)))
    adapter_up_weight = bell_draw(arg_keys[3], (ADAPTER_TOTAL, ADAPTER_RANK, 2 * KEY_VALUE_WIDTH), ADAPTER_RANK ** -0.5, 0.75, ((0, 2), (2, 4)))
    token_row_adapter_keys = jax.random.split(jax.random.fold_in(own_keys[4], 1), TOKENS // ROWS_COL)
    token_row_adapter_turns = jax.random.permutation(jax.random.fold_in(own_keys[4], 3), TOKENS // ROWS_COL)
    token_row_adapter = jax.vmap(lambda own, number: shared_out(jax.random.fold_in(own_keys[4], 2), own, number, ROWS_COL, ADAPTER_TOTAL, 1, CAP, 2))(token_row_adapter_keys, token_row_adapter_turns).reshape((TOKENS, 1))
    adapter_slot_table = jax.random.permutation(arg_keys[5], ADAPTER_TOTAL).astype(jnp.int32)
    return {"tokens": tokens, "base_projection_weight": base_projection_weight, "adapter_down_weight": adapter_down_weight, "adapter_up_weight": adapter_up_weight, "token_row_adapter": token_row_adapter, "adapter_slot_table": adapter_slot_table}


adapter_scale = 0.5


def reference(tokens, base_projection_weight, adapter_down_weight, adapter_up_weight, token_row_adapter, adapter_slot_table):
    base_out = jnp.dot(tokens, base_projection_weight, preferred_element_type=jnp.float32)
    down_weight_per_adapter = adapter_down_weight[adapter_slot_table]
    up_weight_per_adapter = adapter_up_weight[adapter_slot_table]
    blocks = TOKENS // ROWS_COL
    block_rows = tokens.reshape(blocks, ROWS_COL, MODEL_WIDTH)
    block_ids = token_row_adapter.reshape(blocks, ROWS_COL)

    def correct(pair):
        rows_here, adapter_ids = pair
        onehot = (adapter_ids[:, None] == jnp.arange(ADAPTER_TOTAL, dtype=jnp.int32)[None, :]).astype(jnp.int32)
        position = jnp.sum((jnp.cumsum(onehot, axis=0) - 1) * onehot, axis=1).astype(jnp.int32)
        packed = jnp.zeros((ADAPTER_TOTAL, CAP, MODEL_WIDTH), jnp.bfloat16).at[adapter_ids, position].set(rows_here)
        shrink_input = jnp.einsum("gcf,gfr->gcr", packed.astype(jnp.float32), down_weight_per_adapter.astype(jnp.float32)).astype(jnp.bfloat16)
        expand_rows = jnp.einsum("gcr,gro->gco", shrink_input.astype(jnp.float32), up_weight_per_adapter.astype(jnp.float32))
        adapter_update = (adapter_scale * expand_rows).astype(jnp.bfloat16)
        return adapter_update[adapter_ids, position]

    corrections = lax.map(correct, (block_rows, block_ids)).reshape(TOKENS, 2 * KEY_VALUE_WIDTH)
    return (base_out + corrections.astype(jnp.float32)).astype(jnp.bfloat16)
```

```python
import functools

import jax
import jax.numpy as jnp
from jax import lax
from jax.experimental import pallas as pl
from jax.experimental.pallas import tpu as pltpu
from jax.sharding import PartitionSpec as P

MESH = pl.DeviceIdType.MESH
CHUNKS = 4
adapter_scale = 0.5


def kernel(
    n,
    owners,
    ids_ref,
    table_ref,
    tok_ref,
    w_ref,
    down_ref,
    up_ref,
    out_ref,
    got,
    wv,
    dv,
    uv,
    part,
    acc,
    tok_sem,
    w_sem,
    own_sem,
    right_sem,
    left_sem,
    got_sem,
    xs_sem,
    xr_sem,
    ps_sem,
    pr_sem,
):
    z = lax.axis_index("tensor")
    x = lax.axis_index("adapter")
    rows, feats = tok_ref.shape
    width = feats // CHUNKS
    slots, rank, _ = down_ref.shape
    total_slots = owners * slots

    barrier = pltpu.get_barrier_semaphore()
    for d in range(1, n):
        pl.semaphore_signal(
            barrier, inc=1, device_id={"tensor": lax.rem(z + d, n)}, device_id_type=MESH
        )
    for d in range(1, owners):
        pl.semaphore_signal(
            barrier, inc=1, device_id={"adapter": lax.rem(x + d, owners)}, device_id_type=MESH
        )

    tok_copies = []
    for c in range(CHUNKS):
        cp = pltpu.make_async_copy(
            tok_ref.at[:, pl.ds(c * width, width)], got.at[z, c], tok_sem.at[c]
        )
        cp.start()
        tok_copies.append(cp)

    def w_copy(k):
        return pltpu.make_async_copy(
            w_ref.at[pl.ds(pl.multiple_of(k * feats, feats), feats), :], wv.at[k], w_sem.at[k]
        )

    for d in range(n):
        w_copy(lax.rem(z + d, n)).start()
    own_down = pltpu.make_async_copy(down_ref, dv.at[x], own_sem.at[0])
    own_up = pltpu.make_async_copy(up_ref, uv.at[x], own_sem.at[1])
    own_down.start()
    own_up.start()

    pl.semaphore_wait(barrier, n - 1 + owners - 1)

    def send(src, shard, c, to_right):
        return pltpu.make_async_remote_copy(
            src_ref=src,
            dst_ref=got.at[shard, c],
            send_sem=(right_sem if to_right else left_sem).at[shard, c],
            recv_sem=got_sem.at[shard, c],
            device_id={"tensor": z + 1 if to_right else z - 1},
            device_id_type=MESH,
        )

    def own_send(c, to_right):
        return send(tok_ref.at[:, pl.ds(c * width, width)], z, c, to_right)

    def forward(shard, c, to_right):
        return send(got.at[shard, c], shard, c, to_right)

    for c in range(CHUNKS):

        @pl.when(z < n - 1)
        def _():
            own_send(c, True).start()

        @pl.when(z > 0)
        def _():
            own_send(c, False).start()

    def weight_copies(d):
        to = lax.rem(x + d, owners)
        return [
            pltpu.make_async_remote_copy(
                src_ref=src,
                dst_ref=dst.at[x],
                send_sem=xs_sem.at[k, to],
                recv_sem=xr_sem.at[k, x],
                device_id={"adapter": to},
                device_id_type=MESH,
            )
            for k, (src, dst) in enumerate(((down_ref, dv), (up_ref, uv)))
        ]

    for d in range(1, owners):
        for cp in weight_copies(d):
            cp.start()

    def mul(shard, c):
        acc[...] += jnp.dot(
            got[shard, c],
            wv[shard, pl.ds(c * width, width), :],
            preferred_element_type=jnp.float32,
        )

    acc[...] = jnp.zeros_like(acc)
    w_copy(z).wait()
    for c in range(CHUNKS):
        tok_copies[c].wait()
        mul(z, c)
    for d in range(1, n):
        w_copy(lax.rem(z + d, n)).wait()

    def step(t):
        low, high = z - t, z + t
        for c in range(CHUNKS):

            @pl.when(low >= 0)
            def _():
                forward(low, c, True).wait_recv()

                @pl.when(z < n - 1)
                def _():
                    forward(low, c, True).start()

            @pl.when(high < n)
            def _():
                forward(high, c, False).wait_recv()

                @pl.when(z > 0)
                def _():
                    forward(high, c, False).start()

            @pl.when(low >= 0)
            def _():
                mul(low, c)

            @pl.when(high < n)
            def _():
                mul(high, c)

    slot = jnp.zeros(ids_ref.shape, jnp.int32)
    for g in range(total_slots):
        slot = slot + jnp.where(ids_ref[...] == g, table_ref[g], 0)

    def part_copy(d):
        to = lax.rem(z + d, n)
        return pltpu.make_async_remote_copy(
            src_ref=part.at[z],
            dst_ref=part.at[z],
            send_sem=ps_sem.at[to],
            recv_sem=pr_sem.at[z],
            device_id={"tensor": to},
            device_id_type=MESH,
        )

    def arrived(ref, sem):
        pltpu.make_async_copy(ref, ref, sem).wait()

    step(1)

    own_down.wait()
    own_up.wait()
    for d in range(1, owners):
        src = lax.rem(x + d, owners)
        arrived(dv.at[src], xr_sem.at[0, src])
        arrived(uv.at[src], xr_sem.at[1, src])
    own_part = jnp.zeros((rank, rows), jnp.float32)
    for o in range(owners):
        down = dv[o].reshape(slots * rank, feats)
        prod = jnp.zeros((slots * rank, rows), jnp.float32)
        for c in range(CHUNKS):
            prod = prod + lax.dot_general(
                down[:, c * width : (c + 1) * width],
                got[z, c],
                (((1,), (1,)), ((), ())),
                preferred_element_type=jnp.float32,
            )
        for s in range(slots):
            own_part = own_part + jnp.where(
                slot == o * slots + s, prod[s * rank : (s + 1) * rank], 0.0
            )
    part[z] = own_part
    for d in range(1, n):
        part_copy(d).start()

    def middle(t, carry):
        step(t)
        return carry

    lax.fori_loop(2, n - 1, middle, 0)

    for d in range(1, n):
        src = lax.rem(z + d, n)
        arrived(part.at[src], pr_sem.at[src])
    shrink = part[0]
    for k in range(1, n):
        shrink = shrink + part[k]
    shrink = shrink.astype(jnp.bfloat16).astype(jnp.float32)
    spread = jnp.concatenate(
        [jnp.where(slot == k, shrink, 0.0) for k in range(total_slots)], axis=0
    ).astype(jnp.bfloat16)
    delta = lax.dot_general(
        spread,
        uv[...].reshape(total_slots * rank, uv.shape[-1]),
        (((0,), (0,)), ((), ())),
        preferred_element_type=jnp.float32,
    )
    acc[...] += (adapter_scale * delta).astype(jnp.bfloat16).astype(jnp.float32)

    step(n - 1)
    out_ref[...] = acc[...].astype(jnp.bfloat16)

    for c in range(CHUNKS):

        @pl.when(z < n - 1)
        def _():
            own_send(c, True).wait_send()

        @pl.when(z > 0)
        def _():
            own_send(c, False).wait_send()

    def drain(t, carry):
        for c in range(CHUNKS):

            @pl.when(jnp.logical_and(z - t >= 0, z < n - 1))
            def _():
                forward(z - t, c, True).wait_send()

            @pl.when(jnp.logical_and(z + t < n, z > 0))
            def _():
                forward(z + t, c, False).wait_send()

        return carry

    lax.fori_loop(1, n, drain, 0)
    for d in range(1, owners):
        for cp in weight_copies(d):
            cp.wait_send()
    for d in range(1, n):
        part_copy(d).wait_send()


def on_device(
    n,
    owners,
    tokens,
    base_projection_weight,
    adapter_down_weight,
    adapter_up_weight,
    token_row_adapter,
    adapter_slot_table,
):
    rows, feats = tokens.shape
    out_cols = base_projection_weight.shape[1]
    slots, _, rank = adapter_down_weight.shape
    width = feats // CHUNKS
    any_spec = pl.BlockSpec(memory_space=pl.ANY)
    dma = pltpu.SemaphoreType.DMA
    bf16 = jnp.bfloat16
    return pl.pallas_call(
        functools.partial(kernel, n, owners),
        out_shape=jax.ShapeDtypeStruct((rows, out_cols), bf16),
        in_specs=[
            pl.BlockSpec(memory_space=pltpu.VMEM),
            pl.BlockSpec(memory_space=pltpu.SMEM),
            any_spec,
            any_spec,
            any_spec,
            any_spec,
        ],
        out_specs=pl.BlockSpec(memory_space=pltpu.VMEM),
        scratch_shapes=[
            pltpu.VMEM((n, CHUNKS, rows, width), bf16),
            pltpu.VMEM((n, feats, out_cols), bf16),
            pltpu.VMEM((owners, slots, rank, feats), bf16),
            pltpu.VMEM((owners, slots, rank, out_cols), bf16),
            pltpu.VMEM((n, rank, rows), jnp.float32),
            pltpu.VMEM((rows, out_cols), jnp.float32),
            dma((CHUNKS,)),
            dma((n,)),
            dma((2,)),
            dma((n, CHUNKS)),
            dma((n, CHUNKS)),
            dma((n, CHUNKS)),
            dma((2, owners)),
            dma((2, owners)),
            dma((n,)),
            dma((n,)),
        ],
        compiler_params=pltpu.CompilerParams(
            collective_id=0, has_side_effects=True, vmem_limit_bytes=60 * 1024 * 1024
        ),
    )(
        token_row_adapter.T,
        adapter_slot_table,
        tokens,
        base_projection_weight,
        jnp.swapaxes(adapter_down_weight, 1, 2),
        adapter_up_weight,
    )


def solution(mesh):
    in_specs = (
        P(("groups", "adapter", "dp"), "tensor"),
        P(None, "tensor"),
        P("adapter", "tensor", None),
        P("adapter", None, "tensor"),
        P(("groups", "adapter", "dp"), None),
        P(),
    )
    out_specs = P(("groups", "adapter", "dp"), "tensor")
    return jax.shard_map(
        functools.partial(on_device, mesh.shape["tensor"], mesh.shape["adapter"]),
        mesh=mesh,
        in_specs=in_specs,
        out_specs=out_specs,
        check_vma=False,
    )
```

```python
import functools

import jax
import jax.numpy as jnp
from jax import lax
from jax.experimental import pallas as pl
from jax.experimental.pallas import tpu as pltpu
from jax.sharding import PartitionSpec as P

MESH = pl.DeviceIdType.MESH
MOST_CHUNKS = 8
LANES = 128
LAG = 2
adapter_scale = 0.5


def kernel(
    n,
    owners,
    ids_ref,
    table_ref,
    tok_ref,
    w_ref,
    down_ref,
    up_ref,
    out_ref,
    got,
    wv,
    wx,
    dv,
    uv,
    part,
    pout,
    pin,
    acc,
    tok_sem,
    w_sem,
    own_sem,
    right_sem,
    left_sem,
    got_sem,
    ws_sem,
    wy_sem,
    wc_sem,
    wr_sem,
    po_sem,
    xs_sem,
    xr_sem,
    ps_sem,
    pr_sem,
):
    z = lax.axis_index("tensor")
    x = lax.axis_index("adapter")
    y = lax.axis_index("groups")
    core = lax.axis_index("dp")
    rows, feats = tok_ref.shape
    chunks = got.shape[1]
    width = feats // chunks
    slots, rank, _ = down_ref.shape
    total_slots = owners * slots
    quarter = feats // 4
    piece = quarter // chunks

    is_end = jnp.logical_or(z == 0, z == n - 1)
    is_relay = jnp.logical_or(z == 1, z == n - 2)
    relay = jnp.where(z == 0, 1, n - 2)
    end = jnp.where(z == 1, 0, n - 1)

    barrier = pltpu.get_barrier_semaphore()
    peers = [{"tensor": lax.rem(z + d, n)} for d in range(1, n)]
    peers += [{"adapter": lax.rem(x + d, owners)} for d in range(1, owners)]
    peers += [{"groups": 1 - y}, {"dp": 1 - core}]
    for peer in peers:
        pl.semaphore_signal(barrier, inc=1, device_id=peer, device_id_type=MESH)

    tok_copies = []
    for c in range(chunks):
        cp = pltpu.make_async_copy(
            tok_ref.at[:, pl.ds(c * width, width)], got.at[z, c], tok_sem.at[c]
        )
        cp.start()
        tok_copies.append(cp)

    def w_copy(k):
        return pltpu.make_async_copy(
            w_ref.at[pl.ds(pl.multiple_of(k * feats, feats), feats), :], wv.at[k], w_sem.at[k]
        )

    w_copy(z).start()
    pl.semaphore_wait(barrier, len(peers))

    def remote(src, dst, send_sem, recv_sem, to):
        return pltpu.make_async_remote_copy(
            src_ref=src,
            dst_ref=dst,
            send_sem=send_sem,
            recv_sem=recv_sem,
            device_id=to,
            device_id_type=MESH,
        )

    def arrived(ref, sem):
        pltpu.make_async_copy(ref, ref, sem).wait()

    def send(src, shard, c, to_right):
        return remote(
            src,
            got.at[shard, c],
            (right_sem if to_right else left_sem).at[shard, c],
            got_sem.at[shard, c],
            {"tensor": z + 1 if to_right else z - 1},
        )

    def own_send(c, to_right):
        return send(tok_ref.at[:, pl.ds(c * width, width)], z, c, to_right)

    def forward(shard, c, to_right):
        return send(got.at[shard, c], shard, c, to_right)

    inner_right = jnp.logical_and(z > 0, z < n - 2)
    inner_left = jnp.logical_and(z < n - 1, z > 1)

    mine = 2 * y + core
    across = 2 * (1 - y) + core

    def w_piece(q, i):
        return wx.at[q, pl.ds(i * piece, piece), :]

    def w_send(i):
        start = relay * feats + mine * quarter + i * piece
        src = w_ref.at[pl.ds(pl.multiple_of(start, piece), piece), :]
        return remote(
            src, w_piece(mine, i), ws_sem.at[i], wr_sem.at[mine, i], {"tensor": relay}
        )

    def w_across(i):
        src = w_piece(mine, i)
        return remote(src, src, wy_sem.at[i], wr_sem.at[mine, i], {"groups": 1 - y})

    def w_core(q, i):
        src = w_piece(q, i)
        return remote(
            src, src, wc_sem.at[(q - core) // 2, i], wr_sem.at[q, i], {"dp": 1 - core}
        )

    @pl.when(is_end)
    def _():
        for c in range(chunks):
            w_send(c).start()

    for c in range(chunks):

        @pl.when(inner_right)
        def _():
            own_send(c, True).start()

        @pl.when(inner_left)
        def _():
            own_send(c, False).start()

    def weight_copies(d):
        to = lax.rem(x + d, owners)
        return [
            remote(src, dst.at[x], xs_sem.at[k, to], xr_sem.at[k, x], {"adapter": to})
            for k, (src, dst) in enumerate(((down_ref, dv), (up_ref, uv)))
        ]

    for d in range(1, owners):
        for cp in weight_copies(d):
            cp.start()
    own_down = pltpu.make_async_copy(down_ref, dv.at[x], own_sem.at[0])
    own_up = pltpu.make_async_copy(up_ref, uv.at[x], own_sem.at[1])
    own_down.start()
    own_up.start()
    for d in range(1, n):
        w_copy(lax.rem(z + d, n)).start()

    def mul(shard, c):
        acc[...] += jnp.dot(
            got[shard, c],
            wv[shard, pl.ds(c * width, width), :],
            preferred_element_type=jnp.float32,
        )

    def sources(t):
        low = z - t - jnp.where(z == n - 1, 1, 0) + jnp.where(z == 1, 1, 0)
        high = z + t + jnp.where(z == 0, 1, 0) - jnp.where(z == n - 2, 1, 0)
        return low, high, jnp.logical_and(low >= 0, low < z), jnp.logical_and(high < n, high > z)

    def take_low(low, c):
        arrived(got.at[low, c], got_sem.at[low, c])

        @pl.when(z < n - 1)
        def _():
            forward(low, c, True).start()

    def step(t, hook=None, before=None):
        low, high, has_low, has_high = sources(t)
        left_half = z < n // 2
        for c in range(chunks):

            @pl.when(jnp.logical_and(has_low, left_half))
            def _():
                take_low(low, c)

            @pl.when(has_high)
            def _():
                arrived(got.at[high, c], got_sem.at[high, c])

                @pl.when(z > 0)
                def _():
                    forward(high, c, False).start()

            @pl.when(jnp.logical_and(has_low, jnp.logical_not(left_half)))
            def _():
                take_low(low, c)

            if before is not None:
                before(c)

            @pl.when(has_low)
            def _():
                mul(low, c)

            @pl.when(has_high)
            def _():
                mul(high, c)

            if hook is not None:
                hook(c)

    slot = jnp.zeros(ids_ref.shape, jnp.int32)
    for g in range(total_slots):
        slot = slot + jnp.where(ids_ref[...] == g, table_ref[g], 0)

    def part_copy(d):
        to = lax.rem(z + d, n)
        return remote(part.at[z], part.at[z], ps_sem.at[to], pr_sem.at[z], {"tensor": to})

    def own_work():
        acc[...] = jnp.zeros_like(acc)
        w_copy(z).wait()
        for c in range(chunks):
            tok_copies[c].wait()
            mul(z, c)
        for d in range(1, n):
            w_copy(lax.rem(z + d, n)).wait()

    def relay_piece(i):
        arrived(w_piece(mine, i), wr_sem.at[mine, i])
        w_across(i).start()
        w_core(mine, i).start()

    def relay_across(i):
        arrived(w_piece(across, i), wr_sem.at[across, i])
        w_core(across, i).start()

    def first_before(c):
        @pl.when(is_relay)
        def _():
            relay_piece(c)
            if c >= LAG:
                relay_across(c - LAG)

        if c >= chunks - 3:
            at = 2 * (c - chunks + 3)
            to = at + 2 if c < chunks - 1 else chunks

            @pl.when(is_end)
            def _():
                for i in range(at, to):

                    @pl.when(z == 0)
                    def _():
                        own_send(i, True).start()

                    @pl.when(z == n - 1)
                    def _():
                        own_send(i, False).start()

    def second_before(c):
        if c < LAG:

            @pl.when(is_relay)
            def _():
                relay_across(chunks - LAG + c)

    def relay_product():
        other = 1 - core
        for i in range(chunks):
            arrived(w_piece(other, i), wr_sem.at[other, i])
            arrived(w_piece(2 + other, i), wr_sem.at[2 + other, i])
        total = jnp.zeros(acc.shape, jnp.float32)
        per = chunks // 4
        for c in range(chunks):
            total = total + jnp.dot(
                got[z, c],
                wx[c // per, (c % per) * width : (c % per + 1) * width, :],
                preferred_element_type=jnp.float32,
            )
        pout[...] = total.astype(jnp.bfloat16)
        product_copy().start()

    def product_copy():
        return remote(pout, pin, po_sem.at[0], po_sem.at[1], {"tensor": end})

    def shrink_part():
        own_down.wait()
        own_up.wait()
        for d in range(1, owners):
            src = lax.rem(x + d, owners)
            arrived(dv.at[src], xr_sem.at[0, src])
            arrived(uv.at[src], xr_sem.at[1, src])
        own_part = jnp.zeros((rank, rows), jnp.float32)
        for o in range(owners):
            down = dv[o].reshape(slots * rank, feats)
            prod = jnp.zeros((slots * rank, rows), jnp.float32)
            for c in range(chunks):
                prod = prod + lax.dot_general(
                    down[:, c * width : (c + 1) * width],
                    got[z, c],
                    (((1,), (1,)), ((), ())),
                    preferred_element_type=jnp.float32,
                )
            for s in range(slots):
                own_part = own_part + jnp.where(
                    slot == o * slots + s, prod[s * rank : (s + 1) * rank], 0.0
                )
        part[z] = own_part
        for d in range(1, n):
            part_copy(d).start()

    def expand():
        for d in range(1, n):
            src = lax.rem(z + d, n)
            arrived(part.at[src], pr_sem.at[src])
        shrink = part[0]
        for k in range(1, n):
            shrink = shrink + part[k]
        shrink = shrink.astype(jnp.bfloat16).astype(jnp.float32)
        spread = jnp.concatenate(
            [jnp.where(slot == k, shrink, 0.0) for k in range(total_slots)], axis=0
        ).astype(jnp.bfloat16)
        delta = lax.dot_general(
            spread,
            uv[...].reshape(total_slots * rank, uv.shape[-1]),
            (((0,), (0,)), ((), ())),
            preferred_element_type=jnp.float32,
        )
        acc[...] += (adapter_scale * delta).astype(jnp.bfloat16).astype(jnp.float32)

    def second_hook(c):
        if c == 1:
            shrink_part()
        if c == 3:

            @pl.when(is_relay)
            def _():
                relay_product()

        if c == chunks - 2:
            expand()
        if c == max(chunks - 2, 3):

            @pl.when(is_end)
            def _():
                arrived(pin, po_sem.at[1])
                acc[...] += pin[...].astype(jnp.float32)

    own_work()
    step(1, before=first_before)
    step(2, hook=second_hook, before=second_before)

    def later(t, carry):
        step(t)
        return carry

    lax.fori_loop(3, n - 1, later, 0)
    out_ref[...] = acc[...].astype(jnp.bfloat16)

    for c in range(chunks):

        @pl.when(z < n - 2)
        def _():
            own_send(c, True).wait_send()

        @pl.when(z > 1)
        def _():
            own_send(c, False).wait_send()

        @pl.when(is_end)
        def _():
            w_send(c).wait_send()

        @pl.when(is_relay)
        def _():
            w_across(c).wait_send()
            w_core(mine, c).wait_send()
            w_core(across, c).wait_send()

    @pl.when(is_relay)
    def _():
        product_copy().wait_send()

    def drain(t, carry):
        low, high, has_low, has_high = sources(t)
        for c in range(chunks):

            @pl.when(jnp.logical_and(has_low, z < n - 1))
            def _():
                forward(low, c, True).wait_send()

            @pl.when(jnp.logical_and(has_high, z > 0))
            def _():
                forward(high, c, False).wait_send()

        return carry

    lax.fori_loop(1, n - 1, drain, 0)
    for d in range(1, owners):
        for cp in weight_copies(d):
            cp.wait_send()
    for d in range(1, n):
        part_copy(d).wait_send()


def on_device(
    n,
    owners,
    tokens,
    base_projection_weight,
    adapter_down_weight,
    adapter_up_weight,
    token_row_adapter,
    adapter_slot_table,
):
    rows, feats = tokens.shape
    out_cols = base_projection_weight.shape[1]
    slots, _, rank = adapter_down_weight.shape
    chunks = min(MOST_CHUNKS, feats // LANES)
    width = feats // chunks
    any_spec = pl.BlockSpec(memory_space=pl.ANY)
    dma = pltpu.SemaphoreType.DMA
    bf16 = jnp.bfloat16
    return pl.pallas_call(
        functools.partial(kernel, n, owners),
        out_shape=jax.ShapeDtypeStruct((rows, out_cols), bf16),
        in_specs=[
            pl.BlockSpec(memory_space=pltpu.VMEM),
            pl.BlockSpec(memory_space=pltpu.SMEM),
            any_spec,
            any_spec,
            any_spec,
            any_spec,
        ],
        out_specs=pl.BlockSpec(memory_space=pltpu.VMEM),
        scratch_shapes=[
            pltpu.VMEM((n, chunks, rows, width), bf16),
            pltpu.VMEM((n, feats, out_cols), bf16),
            pltpu.VMEM((4, feats // 4, out_cols), bf16),
            pltpu.VMEM((owners, slots, rank, feats), bf16),
            pltpu.VMEM((owners, slots, rank, out_cols), bf16),
            pltpu.VMEM((n, rank, rows), jnp.float32),
            pltpu.VMEM((rows, out_cols), bf16),
            pltpu.VMEM((rows, out_cols), bf16),
            pltpu.VMEM((rows, out_cols), jnp.float32),
            dma((chunks,)),
            dma((n,)),
            dma((2,)),
            dma((n, chunks)),
            dma((n, chunks)),
            dma((n, chunks)),
            dma((chunks,)),
            dma((chunks,)),
            dma((2, chunks)),
            dma((4, chunks)),
            dma((2,)),
            dma((2, owners)),
            dma((2, owners)),
            dma((n,)),
            dma((n,)),
        ],
        compiler_params=pltpu.CompilerParams(
            collective_id=0, has_side_effects=True, vmem_limit_bytes=60 * 1024 * 1024
        ),
    )(
        token_row_adapter.T,
        adapter_slot_table,
        tokens,
        base_projection_weight,
        jnp.swapaxes(adapter_down_weight, 1, 2),
        adapter_up_weight,
    )


def solution(mesh):
    in_specs = (
        P(("groups", "adapter", "dp"), "tensor"),
        P(None, "tensor"),
        P("adapter", "tensor", None),
        P("adapter", None, "tensor"),
        P(("groups", "adapter", "dp"), None),
        P(),
    )
    out_specs = P(("groups", "adapter", "dp"), "tensor")
    return jax.shard_map(
        functools.partial(on_device, mesh.shape["tensor"], mesh.shape["adapter"]),
        mesh=mesh,
        in_specs=in_specs,
        out_specs=out_specs,
        check_vma=False,
    )
```

```python
import functools

import jax
import jax.numpy as jnp
from jax import lax
from jax.experimental import pallas as pl
from jax.experimental.pallas import tpu as pltpu
from jax.sharding import PartitionSpec as P

MESH = pl.DeviceIdType.MESH
CHUNKS = 4
adapter_scale = 0.5


def kernel(
    n,
    owners,
    ids_ref,
    table_ref,
    tok_ref,
    w_ref,
    down_ref,
    up_ref,
    out_ref,
    got,
    wv,
    dv,
    uv,
    part,
    acc,
    tok_sem,
    w_sem,
    own_sem,
    right_sem,
    left_sem,
    got_sem,
    xs_sem,
    xr_sem,
    ps_sem,
    pr_sem,
):
    z = lax.axis_index("tensor")
    x = lax.axis_index("adapter")
    rows, feats = tok_ref.shape
    width = feats // CHUNKS
    slots, rank, _ = down_ref.shape
    total_slots = owners * slots

    barrier = pltpu.get_barrier_semaphore()
    for d in range(1, n):
        pl.semaphore_signal(
            barrier, inc=1, device_id={"tensor": lax.rem(z + d, n)}, device_id_type=MESH
        )
    for d in range(1, owners):
        pl.semaphore_signal(
            barrier, inc=1, device_id={"adapter": lax.rem(x + d, owners)}, device_id_type=MESH
        )

    tok_copies = []
    for c in range(CHUNKS):
        cp = pltpu.make_async_copy(
            tok_ref.at[:, pl.ds(c * width, width)], got.at[z, c], tok_sem.at[c]
        )
        cp.start()
        tok_copies.append(cp)

    def w_copy(k):
        return pltpu.make_async_copy(
            w_ref.at[pl.ds(pl.multiple_of(k * feats, feats), feats), :], wv.at[k], w_sem.at[k]
        )

    for d in range(n):
        w_copy(lax.rem(z + d, n)).start()
    own_down = pltpu.make_async_copy(down_ref, dv.at[x], own_sem.at[0])
    own_up = pltpu.make_async_copy(up_ref, uv.at[x], own_sem.at[1])
    own_down.start()
    own_up.start()

    pl.semaphore_wait(barrier, n - 1 + owners - 1)

    def send(src, shard, c, to_right):
        return pltpu.make_async_remote_copy(
            src_ref=src,
            dst_ref=got.at[shard, c],
            send_sem=(right_sem if to_right else left_sem).at[shard, c],
            recv_sem=got_sem.at[shard, c],
            device_id={"tensor": z + 1 if to_right else z - 1},
            device_id_type=MESH,
        )

    def own_send(c, to_right):
        return send(tok_ref.at[:, pl.ds(c * width, width)], z, c, to_right)

    def forward(shard, c, to_right):
        return send(got.at[shard, c], shard, c, to_right)

    for c in range(CHUNKS):

        @pl.when(z < n - 1)
        def _():
            own_send(c, True).start()

        @pl.when(z > 0)
        def _():
            own_send(c, False).start()

    def weight_copies(d):
        to = lax.rem(x + d, owners)
        return [
            pltpu.make_async_remote_copy(
                src_ref=src,
                dst_ref=dst.at[x],
                send_sem=xs_sem.at[k, to],
                recv_sem=xr_sem.at[k, x],
                device_id={"adapter": to},
                device_id_type=MESH,
            )
            for k, (src, dst) in enumerate(((down_ref, dv), (up_ref, uv)))
        ]

    for d in range(1, owners):
        for cp in weight_copies(d):
            cp.start()

    def mul(shard, c):
        acc[...] += jnp.dot(
            got[shard, c],
            wv[shard, pl.ds(c * width, width), :],
            preferred_element_type=jnp.float32,
        )

    acc[...] = jnp.zeros_like(acc)
    w_copy(z).wait()
    for c in range(CHUNKS):
        tok_copies[c].wait()
        mul(z, c)
    for d in range(1, n):
        w_copy(lax.rem(z + d, n)).wait()

    def step(t):
        low, high = z - t, z + t
        for c in range(CHUNKS):

            @pl.when(low >= 0)
            def _():
                forward(low, c, True).wait_recv()

                @pl.when(z < n - 1)
                def _():
                    forward(low, c, True).start()

            @pl.when(high < n)
            def _():
                forward(high, c, False).wait_recv()

                @pl.when(z > 0)
                def _():
                    forward(high, c, False).start()

            @pl.when(low >= 0)
            def _():
                mul(low, c)

            @pl.when(high < n)
            def _():
                mul(high, c)

    slot = jnp.zeros(ids_ref.shape, jnp.int32)
    for g in range(total_slots):
        slot = slot + jnp.where(ids_ref[...] == g, table_ref[g], 0)

    def part_copy(d):
        to = lax.rem(z + d, n)
        return pltpu.make_async_remote_copy(
            src_ref=part.at[z],
            dst_ref=part.at[z],
            send_sem=ps_sem.at[to],
            recv_sem=pr_sem.at[z],
            device_id={"tensor": to},
            device_id_type=MESH,
        )

    def arrived(ref, sem):
        pltpu.make_async_copy(ref, ref, sem).wait()

    step(1)

    own_down.wait()
    own_up.wait()
    for d in range(1, owners):
        src = lax.rem(x + d, owners)
        arrived(dv.at[src], xr_sem.at[0, src])
        arrived(uv.at[src], xr_sem.at[1, src])
    own_part = jnp.zeros((rank, rows), jnp.float32)
    for o in range(owners):
        down = dv[o].reshape(slots * rank, feats)
        prod = jnp.zeros((slots * rank, rows), jnp.float32)
        for c in range(CHUNKS):
            prod = prod + lax.dot_general(
                down[:, c * width : (c + 1) * width],
                got[z, c],
                (((1,), (1,)), ((), ())),
                preferred_element_type=jnp.float32,
            )
        for s in range(slots):
            own_part = own_part + jnp.where(
                slot == o * slots + s, prod[s * rank : (s + 1) * rank], 0.0
            )
    part[z] = own_part.astype(jnp.bfloat16)
    for d in range(1, n):
        part_copy(d).start()

    def middle(t, carry):
        step(t)
        return carry

    lax.fori_loop(2, n - 1, middle, 0)

    for d in range(1, n):
        src = lax.rem(z + d, n)
        arrived(part.at[src], pr_sem.at[src])
    shrink = part[0].astype(jnp.float32)
    for k in range(1, n):
        shrink = shrink + part[k].astype(jnp.float32)
    shrink = shrink.astype(jnp.bfloat16).astype(jnp.float32)
    spread = jnp.concatenate(
        [jnp.where(slot == k, shrink, 0.0) for k in range(total_slots)], axis=0
    ).astype(jnp.bfloat16)
    delta = lax.dot_general(
        spread,
        uv[...].reshape(total_slots * rank, uv.shape[-1]),
        (((0,), (0,)), ((), ())),
        preferred_element_type=jnp.float32,
    )
    acc[...] += (adapter_scale * delta).astype(jnp.bfloat16).astype(jnp.float32)

    step(n - 1)
    out_ref[...] = acc[...].astype(jnp.bfloat16)

    for c in range(CHUNKS):

        @pl.when(z < n - 1)
        def _():
            own_send(c, True).wait_send()

        @pl.when(z > 0)
        def _():
            own_send(c, False).wait_send()

    def drain(t, carry):
        for c in range(CHUNKS):

            @pl.when(jnp.logical_and(z - t >= 0, z < n - 1))
            def _():
                forward(z - t, c, True).wait_send()

            @pl.when(jnp.logical_and(z + t < n, z > 0))
            def _():
                forward(z + t, c, False).wait_send()

        return carry

    lax.fori_loop(1, n, drain, 0)
    for d in range(1, owners):
        for cp in weight_copies(d):
            cp.wait_send()
    for d in range(1, n):
        part_copy(d).wait_send()


def on_device(
    n,
    owners,
    tokens,
    base_projection_weight,
    adapter_down_weight,
    adapter_up_weight,
    token_row_adapter,
    adapter_slot_table,
):
    rows, feats = tokens.shape
    out_cols = base_projection_weight.shape[1]
    slots, _, rank = adapter_down_weight.shape
    width = feats // CHUNKS
    any_spec = pl.BlockSpec(memory_space=pl.ANY)
    dma = pltpu.SemaphoreType.DMA
    bf16 = jnp.bfloat16
    return pl.pallas_call(
        functools.partial(kernel, n, owners),
        out_shape=jax.ShapeDtypeStruct((rows, out_cols), bf16),
        in_specs=[
            pl.BlockSpec(memory_space=pltpu.VMEM),
            pl.BlockSpec(memory_space=pltpu.SMEM),
            any_spec,
            any_spec,
            any_spec,
            any_spec,
        ],
        out_specs=pl.BlockSpec(memory_space=pltpu.VMEM),
        scratch_shapes=[
            pltpu.VMEM((n, CHUNKS, rows, width), bf16),
            pltpu.VMEM((n, feats, out_cols), bf16),
            pltpu.VMEM((owners, slots, rank, feats), bf16),
            pltpu.VMEM((owners, slots, rank, out_cols), bf16),
            pltpu.VMEM((n, rank, rows), bf16),
            pltpu.VMEM((rows, out_cols), jnp.float32),
            dma((CHUNKS,)),
            dma((n,)),
            dma((2,)),
            dma((n, CHUNKS)),
            dma((n, CHUNKS)),
            dma((n, CHUNKS)),
            dma((2, owners)),
            dma((2, owners)),
            dma((n,)),
            dma((n,)),
        ],
        compiler_params=pltpu.CompilerParams(
            collective_id=0, has_side_effects=True, vmem_limit_bytes=60 * 1024 * 1024
        ),
    )(
        token_row_adapter.T,
        adapter_slot_table,
        tokens,
        base_projection_weight,
        jnp.swapaxes(adapter_down_weight, 1, 2),
        adapter_up_weight,
    )


def solution(mesh):
    in_specs = (
        P(("groups", "adapter", "dp"), "tensor"),
        P(None, "tensor"),
        P("adapter", "tensor", None),
        P("adapter", None, "tensor"),
        P(("groups", "adapter", "dp"), None),
        P(),
    )
    out_specs = P(("groups", "adapter", "dp"), "tensor")
    return jax.shard_map(
        functools.partial(on_device, mesh.shape["tensor"], mesh.shape["adapter"]),
        mesh=mesh,
        in_specs=in_specs,
        out_specs=out_specs,
        check_vma=False,
    )
```
